32 devices in a mesh: row: 8 (over y, x, core), col: 4 (over z).
Axes of the slice: x: 2, y: 2, z: 4, core: 2. Of those that a mesh axis runs over, the one named last changes fastest.
Arguments:
- inputs: bfloat16 [192, 12288], P('row', 'col'), may hold values from -6 to 6
- w_in: bfloat16 [12288, 24576], P('col', 'row'), may hold values from -0.0546875 to 0.0546875
- w_out: bfloat16 [24576, 12288], P('row', 'col'), may hold values from -0.0390625 to 0.0390625
- out_grad: bfloat16 [192, 12288], P('row', 'col'), may hold values from -6 to 6
Outputs:
- output: bfloat16 [192, 12288], P('row', 'col')
- input_grad: bfloat16 [192, 12288], P('row', 'col')
- grad_in_w: bfloat16 [12288, 24576], P('col', 'row')
- grad_out_w: bfloat16 [24576, 12288], P('row', 'col')
The draws below stay inside these ranges and needn't reach their ends.
All inputs are finite; a program needn't handle non-finite values.
Results may differ from the reference program's by a relative error of at most 0.0049.
Values may be sent and summed in bfloat16 or wider, within the bound.
A program may use at most 128 MiB of HBM per device.

```python
import jax
import jax.numpy as jnp
from jax import lax

D = 12288
FF = 24576
TOKENS = 192


def block_scale(key, shape, split, low, high):
    def one(axis_at, shards_of):
        heights = jax.random.uniform(jax.random.fold_in(jax.random.fold_in(key, 6), axis_at), (shards_of,), jnp.float32, low / len(split), high / len(split))
        return jnp.repeat(jnp.exp(heights), shape[axis_at] // shards_of).reshape((-1,) + (1,) * (len(shape) - axis_at - 1))

    factor_of = one(*split[0])
    for cut in split[1:]:
        factor_of = factor_of * one(*cut)
    return factor_of


def gaussian(key, shape, scale, reach, cuts=(), kind=jnp.bfloat16):
    drawn = scale * jax.random.normal(key, shape, jnp.float32)
    if cuts:
        drawn = drawn * block_scale(key, shape, cuts, -0.22, 0.18)
    return jnp.clip(drawn, -reach, reach).astype(kind)


def setup_inputs(seed: int = 0) -> dict:
    splits = jax.random.split(jax.random.key(seed), 5)
    return {
        "inputs": gaussian(splits[0], (TOKENS, D), 1.0, 6.0, ((0, 8), (1, 4))),
        "w_in": gaussian(splits[1], (D, FF), D ** -0.5, 0.0546875, ((0, 4), (1, 8))),
        "w_out": gaussian(splits[2], (FF, D), FF ** -0.5, 0.0390625, ((0, 8), (1, 4))),
        "out_grad": gaussian(splits[3], (TOKENS, D), 1.0, 6.0, ((0, 8), (1, 4))),
    }


gelu_scale = 0.7978845608028654
gelu_cubic = 0.044715


def gelu_parts(hidden):
    inner = gelu_scale * (hidden + gelu_cubic * hidden * hidden * hidden)
    tangent = jnp.tanh(inner)
    value = 0.5 * hidden * (1.0 + tangent)
    slopes = 0.5 * (1.0 + tangent) + 0.5 * hidden * (1.0 - tangent * tangent) * gelu_scale * (1.0 + 3.0 * gelu_cubic * hidden * hidden)
    return value, slopes


def contract_first(left, right):
    return lax.dot_general(left, right, (((0,), (0,)), ((), ())), preferred_element_type=jnp.float32)


def contract_last(left, right):
    return lax.dot_general(left, right, (((1,), (1,)), ((), ())), preferred_element_type=jnp.float32)


def reference(inputs, w_in, w_out, out_grad):
    hidden = jnp.dot(inputs, w_in, preferred_element_type=jnp.float32)
    value, slopes = gelu_parts(hidden)
    activation = value.astype(jnp.bfloat16)
    output = jnp.dot(activation, w_out, preferred_element_type=jnp.float32).astype(jnp.bfloat16)
    act_grad = contract_last(out_grad, w_out)
    hid_grad = (act_grad * slopes).astype(jnp.bfloat16)
    grad_out_w = contract_first(activation, out_grad).astype(jnp.bfloat16)
    grad_in_w = contract_first(inputs, hid_grad).astype(jnp.bfloat16)
    input_grad = contract_last(hid_grad, w_in).astype(jnp.bfloat16)
    return output, input_grad, grad_in_w, grad_out_w
```

```python
import functools

import jax
import jax.numpy as jnp
from jax import lax
from jax.experimental import pallas as pl
from jax.experimental.pallas import tpu as pltpu
from jax.sharding import PartitionSpec as P

gelu_scale = 0.7978845608028654
gelu_cubic = 0.044715
MESH = pl.DeviceIdType.MESH
CHUNK = 256
f32, bf16 = jnp.float32, jnp.bfloat16


def gelu_parts(hidden):
    inner = gelu_scale * (hidden + gelu_cubic * hidden * hidden * hidden)
    tangent = jnp.tanh(inner)
    value = 0.5 * hidden * (1.0 + tangent)
    slopes = 0.5 * (1.0 + tangent) + 0.5 * hidden * (1.0 - tangent * tangent) * gelu_scale * (
        1.0 + 3.0 * gelu_cubic * hidden * hidden
    )
    return (value, slopes)


def contract_first(left, right):
    return lax.dot_general(left, right, (((0,), (0,)), ((), ())), preferred_element_type=f32)


def contract_last(left, right):
    return lax.dot_general(left, right, (((1,), (1,)), ((), ())), preferred_element_type=f32)


def layer_kernel(
    rows, cols, own_in, own_grad, w_in, w_out,
    x, og, act, hg, out_acc, ig_acc,
    slab, win, wout, from_outer, from_inner, to_inner, kept,
    gather_send, gather_recv, share_send, w_sem, outer_sem, inner_sem, in_send, out_send,
):
    row, col = lax.axis_index("row"), lax.axis_index("col")
    chips, half = rows // 2, cols // 2
    chip, core = row // 2, row % 2
    sibling = chip * 2 + (1 - core)
    chunks, tokens = win.shape[0], own_in.shape[0]

    lower = col < half
    inner = jnp.where(lower, col + 1, col - 1)
    outer = jnp.where(lower, col - 1, col + 1)
    away = jnp.where(lower, half - 1 - col, col - half)
    is_mid = away == 0
    has_outer = away < half - 1

    def weight_copies(j):
        cut = pl.ds(pl.multiple_of(j * CHUNK, CHUNK), CHUNK)
        return (
            pltpu.make_async_copy(w_in.at[:, cut], win.at[j], w_sem.at[0, j]),
            pltpu.make_async_copy(w_out.at[cut, :], wout.at[j], w_sem.at[1, j]),
        )

    @pl.loop(0, chunks)
    def _(j):
        for copy in weight_copies(j):
            copy.start()

    barrier = pltpu.get_barrier_semaphore()
    for k in range(1, chips):
        there = lax.rem(chip + k, chips) * 2 + core
        pl.semaphore_signal(barrier, inc=1, device_id=(there, col), device_id_type=MESH)
    pl.semaphore_signal(barrier, inc=1, device_id=(sibling, col), device_id_type=MESH)
    pl.semaphore_signal(barrier, inc=1, device_id=(row, inner), device_id_type=MESH)

    @pl.when(has_outer)
    def _():
        pl.semaphore_signal(barrier, inc=1, device_id=(row, outer), device_id_type=MESH)
        pl.semaphore_wait(barrier, chips + 2)

    @pl.when(jnp.logical_not(has_outer))
    def _():
        pl.semaphore_wait(barrier, chips + 1)

    own = (own_in, own_grad)

    def send_block(a, k):
        there = lax.rem(chip + k, chips) * 2 + core
        return pltpu.make_async_remote_copy(
            src_ref=own[a], dst_ref=slab.at[a, row], send_sem=gather_send.at[a, k],
            recv_sem=gather_recv.at[a, row], device_id=(there, col), device_id_type=MESH,
        )

    def share_block(a, k):
        source = lax.rem(chip + chips - k, chips) * 2 + core
        return pltpu.make_async_remote_copy(
            src_ref=own[a] if k == 0 else slab.at[a, source], dst_ref=slab.at[a, source],
            send_sem=share_send.at[a, k], recv_sem=gather_recv.at[a, source],
            device_id=(sibling, col), device_id_type=MESH,
        )

    def arrived(a, source):
        pltpu.make_async_remote_copy(
            src_ref=own[a], dst_ref=slab.at[a, source], send_sem=gather_send.at[a, 0],
            recv_sem=gather_recv.at[a, source], device_id=(sibling, col), device_id_type=MESH,
        ).wait_recv()

    for a in range(2):
        for k in range(1, chips):
            send_block(a, k).start()
        share_block(a, 0).start()
    for a, (whole, wide) in enumerate(((x, out_acc), (og, ig_acc))):
        for k in range(1, chips):
            arrived(a, lax.rem(chip + chips - k, chips) * 2 + core)
            share_block(a, k).start()
        for k in range(chips):
            arrived(a, lax.rem(chip + chips - k, chips) * 2 + 1 - core)

        def unfold(r, _, a=a, wide=wide):
            at = pl.ds(pl.multiple_of(r * tokens, 8), tokens)

            @pl.when(r == row)
            def _():
                wide[at, :] = own[a][...].astype(f32)

            @pl.when(r != row)
            def _():
                wide[at, :] = slab[a, r].astype(f32)

        lax.fori_loop(0, rows, unfold, None)
        whole[...] = wide[...].astype(bf16)
        wide[...] = jnp.zeros_like(wide)

    def sum_copy(j):
        return pltpu.make_async_remote_copy(
            src_ref=to_inner.at[j], dst_ref=from_outer.at[j], send_sem=in_send.at[j],
            recv_sem=outer_sem.at[j], device_id=(row, inner), device_id_type=MESH,
        )

    def middle_copy(j):
        return pltpu.make_async_remote_copy(
            src_ref=to_inner.at[j], dst_ref=from_inner.at[j], send_sem=in_send.at[j],
            recv_sem=inner_sem.at[j], device_id=(row, inner), device_id_type=MESH,
        )

    def result_copy(j):
        return pltpu.make_async_remote_copy(
            src_ref=from_inner.at[j], dst_ref=from_inner.at[j], send_sem=out_send.at[j],
            recv_sem=inner_sem.at[j], device_id=(row, outer), device_id_type=MESH,
        )

    lag = 1 + 3 * away

    def step(s, _):
        @pl.when(s < chunks)
        def _():
            for copy in weight_copies(s):
                copy.wait()
            slot = lax.rem(s, 2)
            kept[slot, 0] = jnp.dot(x[...], win[s], preferred_element_type=f32)
            kept[slot, 1] = contract_last(og[...], wout[s])

            @pl.when(has_outer)
            def _():
                sum_copy(s).wait_recv()
                kept[slot] = kept[slot] + from_outer[s].astype(f32)

            to_inner[s] = kept[slot].astype(bf16)

            @pl.when(is_mid)
            def _():
                middle_copy(s).start()

            @pl.when(jnp.logical_not(is_mid))
            def _():
                sum_copy(s).start()

        j = s - lag

        @pl.when((j >= 0) & (j < chunks))
        def _():
            middle_copy(j).wait_recv()

            @pl.when(is_mid)
            def _():
                total = kept[lax.rem(j, 2)] + from_inner[j].astype(f32)
                value, slopes = gelu_parts(total[0])
                from_inner[j, 0] = value.astype(bf16)
                from_inner[j, 1] = (total[1] * slopes).astype(bf16)

            @pl.when(has_outer)
            def _():
                result_copy(j).start()

            cut = pl.ds(pl.multiple_of(j * CHUNK, CHUNK), CHUNK)
            act[:, cut] = from_inner[j, 0]
            hg[:, cut] = from_inner[j, 1]
            out_acc[...] += jnp.dot(from_inner[j, 0], wout[j], preferred_element_type=f32)
            ig_acc[...] += contract_last(from_inner[j, 1], win[j])

    lax.fori_loop(0, chunks + 1 + 3 * (half - 1), step, None)

    for a in range(2):
        for k in range(1, chips):
            send_block(a, k).wait_send()
        for k in range(chips):
            share_block(a, k).wait_send()

    @pl.loop(0, chunks)
    def _(j):
        sum_copy(j).wait_send()

        @pl.when(has_outer)
        def _():
            result_copy(j).wait_send()


def layer(rows, cols, inputs, out_grad, w_in, w_out):
    tokens, feats = inputs.shape
    units = w_in.shape[1]
    chunks, batch = units // CHUNK, rows * tokens
    vmem = pl.BlockSpec(memory_space=pltpu.VMEM)
    far = pl.BlockSpec(memory_space=pl.ANY)
    dma = pltpu.SemaphoreType.DMA
    piece = (chunks, 2, batch, CHUNK)
    return pl.pallas_call(
        functools.partial(layer_kernel, rows, cols),
        out_shape=(
            jax.ShapeDtypeStruct((batch, feats), bf16),
            jax.ShapeDtypeStruct((batch, feats), bf16),
            jax.ShapeDtypeStruct((batch, units), bf16),
            jax.ShapeDtypeStruct((batch, units), bf16),
            jax.ShapeDtypeStruct((batch, feats), f32),
            jax.ShapeDtypeStruct((batch, feats), f32),
        ),
        in_specs=[vmem, vmem, far, far],
        out_specs=[vmem] * 6,
        scratch_shapes=[
            pltpu.VMEM((2, rows, tokens, feats), bf16),
            pltpu.VMEM((chunks, feats, CHUNK), bf16),
            pltpu.VMEM((chunks, CHUNK, feats), bf16),
            pltpu.VMEM(piece, bf16),
            pltpu.VMEM(piece, bf16),
            pltpu.VMEM(piece, bf16),
            pltpu.VMEM((2, 2, batch, CHUNK), f32),
            dma((2, rows // 2)),
            dma((2, rows)),
            dma((2, rows // 2)),
            dma((2, chunks)),
            dma((chunks,)),
            dma((chunks,)),
            dma((chunks,)),
            dma((chunks,)),
        ],
        compiler_params=pltpu.CompilerParams(
            collective_id=0, has_side_effects=True, vmem_limit_bytes=64 * 1024 * 1024 - 65536
        ),
        cost_estimate=pl.CostEstimate(
            flops=8 * batch * feats * units, bytes_accessed=4 * feats * units, transcendentals=0
        ),
    )(inputs, out_grad, w_in, w_out)


def grad_kernel(left, right, out):
    out[...] = contract_first(left[...], right[...]).astype(bf16)


def weight_grad(left, right):
    batch, height = left.shape
    width = right.shape[1]
    return pl.pallas_call(
        grad_kernel,
        grid=(height // CHUNK,),
        out_shape=jax.ShapeDtypeStruct((height, width), bf16),
        in_specs=[
            pl.BlockSpec((batch, CHUNK), lambda i: (0, i)),
            pl.BlockSpec((batch, width), lambda i: (0, 0)),
        ],
        out_specs=pl.BlockSpec((CHUNK, width), lambda i: (i, 0)),
        compiler_params=pltpu.CompilerParams(vmem_limit_bytes=32 * 1024 * 1024),
        cost_estimate=pl.CostEstimate(
            flops=2 * batch * height * width, bytes_accessed=2 * height * width, transcendentals=0
        ),
    )(left, right)


def local(rows, cols, inputs, w_in, w_out, out_grad):
    tokens, feats = inputs.shape
    chips = rows // 2
    x, og, act, hg, out_part, ig_part = layer(rows, cols, inputs, out_grad, w_in, w_out)
    row = lax.axis_index("row")
    chip, core = row // 2, row % 2

    parts = jnp.stack((out_part, ig_part)).reshape(2, chips, 2, tokens, feats)
    mine = lax.dynamic_index_in_dim(parts, core, 2, keepdims=False)
    theirs = lax.dynamic_index_in_dim(parts, 1 - core, 2, keepdims=False)
    pairs = [(r, r ^ 1) for r in range(rows)]
    summed = mine + lax.ppermute(theirs, "row", pairs)
    total = lax.dynamic_index_in_dim(summed, chip, 1, keepdims=False)
    for k in range(1, chips):
        block = lax.dynamic_index_in_dim(summed, (chip + k) % chips, 1, keepdims=False)
        shift = [(r, (r + 2 * k) % rows) for r in range(rows)]
        total = total + lax.ppermute(block.astype(bf16), "row", shift).astype(f32)
    total = total.astype(bf16)

    grad_out_w = weight_grad(act, og)
    grad_in_w = weight_grad(x, hg)
    return (total[0], total[1], grad_in_w, grad_out_w)


def solution(mesh):
    placed = (P("row", "col"), P("col", "row"), P("row", "col"), P("row", "col"))
    return jax.shard_map(
        functools.partial(local, mesh.shape["row"], mesh.shape["col"]),
        mesh=mesh,
        in_specs=placed,
        out_specs=(P("row", "col"), P("row", "col"), P("col", "row"), P("row", "col")),
        check_vma=False,
    )
```

```python
import functools

import jax
import jax.numpy as jnp
from jax import lax
from jax.experimental import pallas as pl
from jax.experimental.pallas import tpu as pltpu
from jax.sharding import PartitionSpec as P

gelu_scale = 0.7978845608028654
gelu_cubic = 0.044715
MESH = pl.DeviceIdType.MESH
CHUNK = 256
BLOCK = 768
f32, bf16 = jnp.float32, jnp.bfloat16


def gelu_parts(hidden):
    inner = gelu_scale * (hidden + gelu_cubic * hidden * hidden * hidden)
    tangent = jnp.tanh(inner)
    value = 0.5 * hidden * (1.0 + tangent)
    slopes = 0.5 * (1.0 + tangent) + 0.5 * hidden * (1.0 - tangent * tangent) * gelu_scale * (
        1.0 + 3.0 * gelu_cubic * hidden * hidden
    )
    return (value, slopes)


def contract_first(left, right):
    return lax.dot_general(left, right, (((0,), (0,)), ((), ())), preferred_element_type=f32)


def contract_last(left, right):
    return lax.dot_general(left, right, (((1,), (1,)), ((), ())), preferred_element_type=f32)


def layer_kernel(
    rows, cols, own_in, own_grad, w_in, w_out, *refs
):
    (x_far, og_far, act, hg, own_sum), others = refs[:5], refs[5 : 4 + rows // 2]
    (
        x, og, out_acc, ig_acc, pair,
        slab, win, wout, from_outer, from_inner, to_inner, kept, early,
        gather_send, gather_recv, share_send, w_sem, outer_sem, inner_sem, in_send, out_send,
        far_sem, act_sem, pair_send, pair_recv,
    ) = refs[4 + rows // 2 :]
    row, col = lax.axis_index("row"), lax.axis_index("col")
    chips, half = rows // 2, cols // 2
    chip, core = row // 2, row % 2
    sibling = chip * 2 + (1 - core)
    chunks, tokens = win.shape[0], own_in.shape[0]

    lower = col < half
    inner = jnp.where(lower, col + 1, col - 1)
    outer = jnp.where(lower, col - 1, col + 1)
    away = jnp.where(lower, half - 1 - col, col - half)
    is_mid = away == 0
    has_outer = away < half - 1

    def weight_copies(j):
        cut = pl.ds(pl.multiple_of(j * CHUNK, CHUNK), CHUNK)
        return (
            pltpu.make_async_copy(w_in.at[:, cut], win.at[j], w_sem.at[0, j]),
            pltpu.make_async_copy(w_out.at[cut, :], wout.at[j], w_sem.at[1, j]),
        )

    @pl.loop(0, chunks)
    def _(j):
        for copy in weight_copies(j):
            copy.start()

    barrier = pltpu.get_barrier_semaphore()
    for k in range(1, chips):
        there = lax.rem(chip + k, chips) * 2 + core
        pl.semaphore_signal(barrier, inc=1, device_id=(there, col), device_id_type=MESH)
    pl.semaphore_signal(barrier, inc=1, device_id=(sibling, col), device_id_type=MESH)
    pl.semaphore_signal(barrier, inc=1, device_id=(row, inner), device_id_type=MESH)

    @pl.when(has_outer)
    def _():
        pl.semaphore_signal(barrier, inc=1, device_id=(row, outer), device_id_type=MESH)
        pl.semaphore_wait(barrier, chips + 2)

    @pl.when(jnp.logical_not(has_outer))
    def _():
        pl.semaphore_wait(barrier, chips + 1)

    own = (own_in, own_grad)

    def send_block(a, k):
        there = lax.rem(chip + k, chips) * 2 + core
        return pltpu.make_async_remote_copy(
            src_ref=own[a], dst_ref=slab.at[a, row], send_sem=gather_send.at[a, k],
            recv_sem=gather_recv.at[a, row], device_id=(there, col), device_id_type=MESH,
        )

    def share_block(a, k):
        source = lax.rem(chip + chips - k, chips) * 2 + core
        return pltpu.make_async_remote_copy(
            src_ref=own[a] if k == 0 else slab.at[a, source], dst_ref=slab.at[a, source],
            send_sem=share_send.at[a, k], recv_sem=gather_recv.at[a, source],
            device_id=(sibling, col), device_id_type=MESH,
        )

    def arrived(a, source):
        pltpu.make_async_remote_copy(
            src_ref=own[a], dst_ref=slab.at[a, source], send_sem=gather_send.at[a, 0],
            recv_sem=gather_recv.at[a, source], device_id=(sibling, col), device_id_type=MESH,
        ).wait_recv()

    def far_copy(a):
        return pltpu.make_async_copy((x, og)[a], (x_far, og_far)[a], far_sem.at[a])

    def early_step(s, _):
        weight_copies(s)[0].wait()
        early[s] = jnp.dot(x[...], win[s], preferred_element_type=f32)

    for k in range(1, chips):
        send_block(0, k).start()
    share_block(0, 0).start()
    for k in range(1, chips):
        send_block(0, k).wait_send()
    for k in range(1, chips):
        send_block(1, k).start()
    share_block(1, 0).start()
    for a, (whole, wide) in enumerate(((x, out_acc), (og, ig_acc))):
        for k in range(1, chips):
            arrived(a, lax.rem(chip + chips - k, chips) * 2 + core)
            share_block(a, k).start()
        for k in range(chips):
            arrived(a, lax.rem(chip + chips - k, chips) * 2 + 1 - core)

        def unfold(r, _, a=a, wide=wide):
            at = pl.ds(pl.multiple_of(r * tokens, 8), tokens)

            @pl.when(r == row)
            def _():
                wide[at, :] = own[a][...].astype(f32)

            @pl.when(r != row)
            def _():
                wide[at, :] = slab[a, r].astype(f32)

        lax.fori_loop(0, rows, unfold, None)
        whole[...] = wide[...].astype(bf16)
        wide[...] = jnp.zeros_like(wide)
        far_copy(a).start()
        if a == 0:
            lax.fori_loop(0, early.shape[0], early_step, None)

    def sum_copy(j):
        return pltpu.make_async_remote_copy(
            src_ref=to_inner.at[j], dst_ref=from_outer.at[j], send_sem=in_send.at[j],
            recv_sem=outer_sem.at[j], device_id=(row, inner), device_id_type=MESH,
        )

    def middle_copy(j):
        return pltpu.make_async_remote_copy(
            src_ref=to_inner.at[j], dst_ref=from_inner.at[j], send_sem=in_send.at[j],
            recv_sem=inner_sem.at[j], device_id=(row, inner), device_id_type=MESH,
        )

    def result_copy(j):
        return pltpu.make_async_remote_copy(
            src_ref=from_inner.at[j], dst_ref=from_inner.at[j], send_sem=out_send.at[j],
            recv_sem=inner_sem.at[j], device_id=(row, outer), device_id_type=MESH,
        )

    def act_copies(j):
        cut = pl.ds(pl.multiple_of(j * CHUNK, CHUNK), CHUNK)
        return tuple(
            pltpu.make_async_copy(from_inner.at[j, a], far.at[:, cut], act_sem.at[a, j])
            for a, far in enumerate((act, hg))
        )

    def token_rows(q, which):
        return pl.ds(pl.multiple_of((q * 2 + which) * tokens, 8), tokens)

    def pair_copy(a, q):
        return pltpu.make_async_remote_copy(
            src_ref=(out_acc, ig_acc)[a].at[token_rows(q, 1 - core), :], dst_ref=pair.at[a, q],
            send_sem=pair_send.at[a, q], recv_sem=pair_recv.at[a, q],
            device_id=(sibling, col), device_id_type=MESH,
        )

    lag = 1 + 3 * away

    def step(s, _):
        @pl.when(s < chunks)
        def _():
            weight_copies(s)[1].wait()
            slot = lax.rem(s, 2)

            @pl.when(s < early.shape[0])
            def _():
                kept[slot, 0] = early[s]

            @pl.when(s >= early.shape[0])
            def _():
                weight_copies(s)[0].wait()
                kept[slot, 0] = jnp.dot(x[...], win[s], preferred_element_type=f32)

            kept[slot, 1] = contract_last(og[...], wout[s])

            @pl.when(has_outer)
            def _():
                sum_copy(s).wait_recv()
                kept[slot] = kept[slot] + from_outer[s].astype(f32)

            to_inner[s] = kept[slot].astype(bf16)

            @pl.when(is_mid)
            def _():
                middle_copy(s).start()

            @pl.when(jnp.logical_not(is_mid))
            def _():
                sum_copy(s).start()

        j = s - lag

        @pl.when((j >= 0) & (j < chunks))
        def _():
            middle_copy(j).wait_recv()

            @pl.when(is_mid)
            def _():
                total = kept[lax.rem(j, 2)] + from_inner[j].astype(f32)
                value, slopes = gelu_parts(total[0])
                from_inner[j, 0] = value.astype(bf16)
                from_inner[j, 1] = (total[1] * slopes).astype(bf16)

            @pl.when(has_outer)
            def _():
                result_copy(j).start()

            for copy in act_copies(j):
                copy.start()
            out_acc[...] += jnp.dot(from_inner[j, 0], wout[j], preferred_element_type=f32)

            @pl.when(j == chunks - 1)
            def _():
                for q in range(chips):
                    pair_copy(0, q).start()

            ig_acc[...] += contract_last(from_inner[j, 1], win[j])

    lax.fori_loop(0, chunks + 1 + 3 * (half - 1), step, None)

    for q in range(chips):
        pair_copy(1, q).start()
    for a, acc in enumerate((out_acc, ig_acc)):
        for q in range(chips):
            pair_copy(a, q).wait_recv()
        for k in range(chips):
            q = lax.rem(chip + k, chips)
            block = acc[token_rows(q, core), :] + pair[a, q]
            if k == 0:
                own_sum[a] = block
            else:
                others[k - 1][a] = block.astype(bf16)
        for q in range(chips):
            pair_copy(a, q).wait_send()

    for a in range(2):
        far_copy(a).wait()
        if a == 1:
            for k in range(1, chips):
                send_block(a, k).wait_send()
        for k in range(chips):
            share_block(a, k).wait_send()

    @pl.loop(0, chunks)
    def _(j):
        sum_copy(j).wait_send()
        for copy in act_copies(j):
            copy.wait()

        @pl.when(has_outer)
        def _():
            result_copy(j).wait_send()


def layer(rows, cols, inputs, out_grad, w_in, w_out):
    tokens, feats = inputs.shape
    units = w_in.shape[1]
    chunks, batch = units // CHUNK, rows * tokens
    vmem = pl.BlockSpec(memory_space=pltpu.VMEM)
    far = pl.BlockSpec(memory_space=pl.ANY)
    dma = pltpu.SemaphoreType.DMA
    piece = (chunks, 2, batch, CHUNK)
    return pl.pallas_call(
        functools.partial(layer_kernel, rows, cols),
        out_shape=(
            jax.ShapeDtypeStruct((batch, feats), bf16),
            jax.ShapeDtypeStruct((batch, feats), bf16),
            jax.ShapeDtypeStruct((batch, units), bf16),
            jax.ShapeDtypeStruct((batch, units), bf16),
            jax.ShapeDtypeStruct((2, tokens, feats), f32),
        )
        + (jax.ShapeDtypeStruct((2, tokens, feats), bf16),) * (rows // 2 - 1),
        in_specs=[vmem, vmem, far, far],
        out_specs=[far] * 4 + [vmem] * (rows // 2),
        scratch_shapes=[
            pltpu.VMEM((batch, feats), bf16),
            pltpu.VMEM((batch, feats), bf16),
            pltpu.VMEM((batch, feats), f32),
            pltpu.VMEM((batch, feats), f32),
            pltpu.VMEM((2, rows // 2, tokens, feats), f32),
            pltpu.VMEM((2, rows, tokens, feats), bf16),
            pltpu.VMEM((chunks, feats, CHUNK), bf16),
            pltpu.VMEM((chunks, CHUNK, feats), bf16),
            pltpu.VMEM(piece, bf16),
            pltpu.VMEM(piece, bf16),
            pltpu.VMEM(piece, bf16),
            pltpu.VMEM((2, 2, batch, CHUNK), f32),
            pltpu.VMEM(((chunks + 1) // 2, batch, CHUNK), f32),
            dma((2, rows // 2)),
            dma((2, rows)),
            dma((2, rows // 2)),
            dma((2, chunks)),
            dma((chunks,)),
            dma((chunks,)),
            dma((chunks,)),
            dma((chunks,)),
            dma((2,)),
            dma((2, chunks)),
            dma((2, rows // 2)),
            dma((2, rows // 2)),
        ],
        compiler_params=pltpu.CompilerParams(
            collective_id=0, has_side_effects=True, vmem_limit_bytes=64 * 1024 * 1024 - 65536
        ),
        cost_estimate=pl.CostEstimate(
            flops=8 * batch * feats * units, bytes_accessed=4 * feats * units, transcendentals=0
        ),
    )(inputs, out_grad, w_in, w_out)


def grad_rows_kernel(left, right, out):
    out[...] = contract_first(left[...], right[...]).astype(bf16)


def grad_columns_kernel(left, right, out, turned):
    @pl.when(pl.program_id(0) == 0)
    def _():
        turned[...] = left[...].T

    out[...] = jnp.dot(turned[...], right[...], preferred_element_type=f32).astype(bf16)


def weight_grad(left, right, by_rows):
    batch, height = left.shape
    width = right.shape[1]
    if by_rows:
        grid, body, scratch = height // BLOCK, grad_rows_kernel, []
        in_specs = [
            pl.BlockSpec((batch, BLOCK), lambda i: (0, i)),
            pl.BlockSpec((batch, width), lambda i: (0, 0)),
        ]
        out_specs = pl.BlockSpec((BLOCK, width), lambda i: (i, 0))
    else:
        grid, body, scratch = width // CHUNK, grad_columns_kernel, [pltpu.VMEM((height, batch), bf16)]
        in_specs = [
            pl.BlockSpec((batch, height), lambda i: (0, 0)),
            pl.BlockSpec((batch, CHUNK), lambda i: (0, i)),
        ]
        out_specs = pl.BlockSpec((height, CHUNK), lambda i: (0, i))
    return pl.pallas_call(
        body,
        grid=(grid,),
        out_shape=jax.ShapeDtypeStruct((height, width), bf16),
        in_specs=in_specs,
        out_specs=out_specs,
        scratch_shapes=scratch,
        compiler_params=pltpu.CompilerParams(vmem_limit_bytes=48 * 1024 * 1024),
        cost_estimate=pl.CostEstimate(
            flops=2 * batch * height * width, bytes_accessed=2 * height * width, transcendentals=0
        ),
    )(left, right)


def local(rows, cols, inputs, w_in, w_out, out_grad):
    tokens, feats = inputs.shape
    chips = rows // 2
    x, og, act, hg, total, *blocks = layer(rows, cols, inputs, out_grad, w_in, w_out)

    for k in range(1, chips):
        shift = [(r, (r + 2 * k) % rows) for r in range(rows)]
        total = total + lax.ppermute(blocks[k - 1], "row", shift).astype(f32)
    total = total.astype(bf16)

    grad_out_w = weight_grad(act, og, True)
    grad_in_w = weight_grad(x, hg, False)
    return (total[0], total[1], grad_in_w, grad_out_w)


def solution(mesh):
    placed = (P("row", "col"), P("col", "row"), P("row", "col"), P("row", "col"))
    return jax.shard_map(
        functools.partial(local, mesh.shape["row"], mesh.shape["col"]),
        mesh=mesh,
        in_specs=placed,
        out_specs=(P("row", "col"), P("row", "col"), P("col", "row"), P("row", "col")),
        check_vma=False,
    )
```

```python
import functools

import jax
import jax.numpy as jnp
from jax import lax
from jax.experimental import pallas as pl
from jax.experimental.pallas import tpu as pltpu
from jax.sharding import PartitionSpec as P

gelu_scale = 0.7978845608028654
gelu_cubic = 0.044715
MESH = pl.DeviceIdType.MESH
CHUNK = 256
VMEM_BYTES = 64 * 1024 * 1024 - 65536
f32, bf16 = jnp.float32, jnp.bfloat16


def gelu_parts(hidden):
    inner = gelu_scale * (hidden + gelu_cubic * hidden * hidden * hidden)
    tangent = jnp.tanh(inner)
    value = 0.5 * hidden * (1.0 + tangent)
    slopes = 0.5 * (1.0 + tangent) + 0.5 * hidden * (1.0 - tangent * tangent) * gelu_scale * (
        1.0 + 3.0 * gelu_cubic * hidden * hidden
    )
    return (value, slopes)


def contract_first(left, right):
    return lax.dot_general(left, right, (((0,), (0,)), ((), ())), preferred_element_type=f32)


def contract_last(left, right):
    return lax.dot_general(left, right, (((1,), (1,)), ((), ())), preferred_element_type=f32)


def layer_kernel(
    rows, cols, own_in, own_grad, w_in, w_out, *refs
):
    (x_far, og_far, act, hg, own_sum), others = refs[:5], refs[5 : 4 + rows // 2]
    (
        x, og, out_acc, ig_acc, pair,
        slab, win, wout, from_outer, from_inner, to_inner, kept, early,
        gather_send, gather_recv, share_send, w_sem, outer_sem, inner_sem, in_send, out_send,
        far_sem, act_sem, pair_send, pair_recv,
    ) = refs[4 + rows // 2 :]
    row, col = lax.axis_index("row"), lax.axis_index("col")
    chips, half = rows // 2, cols // 2
    chip, core = row // 2, row % 2
    sibling = chip * 2 + (1 - core)
    chunks, tokens = from_inner.shape[0], own_in.shape[0]
    group = chunks // win.shape[0]
    passed = early.shape[0] // 2

    lower = col < half
    inner = jnp.where(lower, col + 1, col - 1)
    outer = jnp.where(lower, col - 1, col + 1)
    away = jnp.where(lower, half - 1 - col, col - half)
    is_mid = away == 0
    has_outer = away < half - 1

    def units(j):
        return pl.ds(pl.multiple_of(j * CHUNK, CHUNK), CHUNK)

    def w_in_copy(j):
        to = win.at[j // group, :, units(j % group)]
        return pltpu.make_async_copy(w_in.at[:, units(j)], to, w_sem.at[0, j])

    def w_out_copy(j):
        to = wout.at[j // group, units(j % group), :]
        return pltpu.make_async_copy(w_out.at[units(j), :], to, w_sem.at[1, j])

    barrier = pltpu.get_barrier_semaphore()
    for k in range(1, chips):
        there = lax.rem(chip + k, chips) * 2 + core
        pl.semaphore_signal(barrier, inc=1, device_id=(there, col), device_id_type=MESH)
    pl.semaphore_signal(barrier, inc=1, device_id=(sibling, col), device_id_type=MESH)
    pl.semaphore_signal(barrier, inc=1, device_id=(row, inner), device_id_type=MESH)

    @pl.when(has_outer)
    def _():
        pl.semaphore_signal(barrier, inc=1, device_id=(row, outer), device_id_type=MESH)

    @pl.loop(0, chunks)
    def _(j):
        w_in_copy(j).start()
        w_out_copy(j).start()

    @pl.when(has_outer)
    def _():
        pl.semaphore_wait(barrier, chips + 2)

    @pl.when(jnp.logical_not(has_outer))
    def _():
        pl.semaphore_wait(barrier, chips + 1)

    own = (own_in, own_grad)

    def send_block(a, k):
        there = lax.rem(chip + k, chips) * 2 + core
        return pltpu.make_async_remote_copy(
            src_ref=own[a], dst_ref=slab.at[a, row], send_sem=gather_send.at[a, k],
            recv_sem=gather_recv.at[a, row], device_id=(there, col), device_id_type=MESH,
        )

    def share_block(a, k):
        source = lax.rem(chip + chips - k, chips) * 2 + core
        return pltpu.make_async_remote_copy(
            src_ref=own[a] if k == 0 else slab.at[a, source], dst_ref=slab.at[a, source],
            send_sem=share_send.at[a, k], recv_sem=gather_recv.at[a, source],
            device_id=(sibling, col), device_id_type=MESH,
        )

    def arrived(a, source):
        pltpu.make_async_remote_copy(
            src_ref=own[a], dst_ref=slab.at[a, source], send_sem=gather_send.at[a, 0],
            recv_sem=gather_recv.at[a, source], device_id=(sibling, col), device_id_type=MESH,
        ).wait_recv()

    def far_copy(a):
        return pltpu.make_async_copy((x, og)[a], (x_far, og_far)[a], far_sem.at[a])

    def sum_copy(a, j):
        return pltpu.make_async_remote_copy(
            src_ref=to_inner.at[j, a], dst_ref=from_outer.at[j, a], send_sem=in_send.at[a, j],
            recv_sem=outer_sem.at[a, j], device_id=(row, inner), device_id_type=MESH,
        )

    def middle_copy(a, j):
        return pltpu.make_async_remote_copy(
            src_ref=to_inner.at[j, a], dst_ref=from_inner.at[j, a], send_sem=in_send.at[a, j],
            recv_sem=inner_sem.at[a, j], device_id=(row, inner), device_id_type=MESH,
        )

    def result_copy(a, j):
        return pltpu.make_async_remote_copy(
            src_ref=from_inner.at[j, a], dst_ref=from_inner.at[j, a], send_sem=out_send.at[a, j],
            recv_sem=inner_sem.at[a, j], device_id=(row, outer), device_id_type=MESH,
        )

    def pass_inward(a, j, part):
        @pl.when(has_outer)
        def _():
            sum_copy(a, j).wait_recv()
            part[...] = part[...] + from_outer[j, a].astype(f32)

        to_inner[j, a] = part[...].astype(bf16)

        @pl.when(is_mid)
        def _():
            middle_copy(a, j).start()

        @pl.when(jnp.logical_not(is_mid))
        def _():
            sum_copy(a, j).start()

    def hidden_part(s):
        w_in_copy(s).wait()
        return jnp.dot(x[...], win[s // group, :, units(s % group)], preferred_element_type=f32)

    def early_step(s, _):
        early[s] = hidden_part(s)

        @pl.when(jnp.logical_not(has_outer))
        def _():
            pass_inward(0, s, early.at[s])

    def early_pass(s, _):
        @pl.when(has_outer)
        def _():
            pass_inward(0, s, early.at[s])

    for k in range(1, chips):
        send_block(0, k).start()
    share_block(0, 0).start()
    for k in range(1, chips):
        send_block(0, k).wait_send()
    for k in range(1, chips):
        send_block(1, k).start()
    share_block(1, 0).start()
    for a, (whole, wide) in enumerate(((x, out_acc), (og, ig_acc))):
        for k in range(1, chips):
            arrived(a, lax.rem(chip + chips - k, chips) * 2 + core)
            share_block(a, k).start()
        for k in range(chips):
            arrived(a, lax.rem(chip + chips - k, chips) * 2 + 1 - core)

        def unfold(r, _, a=a, wide=wide):
            at = pl.ds(pl.multiple_of(r * tokens, 8), tokens)

            @pl.when(r == row)
            def _():
                wide[at, :] = own[a][...].astype(f32)

            @pl.when(r != row)
            def _():
                wide[at, :] = slab[a, r].astype(f32)

        lax.fori_loop(0, rows, unfold, None)
        whole[...] = wide[...].astype(bf16)
        wide[...] = jnp.zeros_like(wide)
        far_copy(a).start()
        if a == 0:
            lax.fori_loop(0, early.shape[0], early_step, None)
            lax.fori_loop(0, passed, early_pass, None)

    def act_copies(j):
        return tuple(
            pltpu.make_async_copy(from_inner.at[j, a], far.at[:, units(j)], act_sem.at[a, j])
            for a, far in enumerate((act, hg))
        )

    def token_rows(q, which):
        return pl.ds(pl.multiple_of((q * 2 + which) * tokens, 8), tokens)

    def pair_copy(a, q):
        return pltpu.make_async_remote_copy(
            src_ref=(out_acc, ig_acc)[a].at[token_rows(q, 1 - core), :], dst_ref=pair.at[a, q],
            send_sem=pair_send.at[a, q], recv_sem=pair_recv.at[a, q],
            device_id=(sibling, col), device_id_type=MESH,
        )

    lag = 1 + 3 * away

    def step(s, _):
        @pl.when(s < chunks)
        def _():
            slot = lax.rem(s, 2)

            @pl.when(s < early.shape[0])
            def _():
                @pl.when(has_outer & (s >= passed))
                def _():
                    pass_inward(0, s, early.at[s])

                kept[slot, 0] = early[s]

            @pl.when(s >= early.shape[0])
            def _():
                kept[slot, 0] = hidden_part(s)
                pass_inward(0, s, kept.at[slot, 0])

            w_out_copy(s).wait()
            kept[slot, 1] = contract_last(og[...], wout[s // group, units(s % group), :])
            pass_inward(1, s, kept.at[slot, 1])

        j = s - lag

        @pl.when((j >= 0) & (j < chunks))
        def _():
            middle_copy(0, j).wait_recv()
            middle_copy(1, j).wait_recv()

            @pl.when(is_mid)
            def _():
                total = kept[lax.rem(j, 2)] + from_inner[j].astype(f32)
                value, slopes = gelu_parts(total[0])
                from_inner[j, 0] = value.astype(bf16)
                from_inner[j, 1] = (total[1] * slopes).astype(bf16)

            @pl.when(has_outer)
            def _():
                result_copy(0, j).start()
                result_copy(1, j).start()

            for copy in act_copies(j):
                copy.start()

            @pl.when(lax.rem(j, group) == group - 1)
            def _():
                g = j // group

                def gathered(a):
                    return jnp.concatenate(
                        [from_inner[g * group + i, a] for i in range(group)], axis=1
                    )

                out_acc[...] += jnp.dot(gathered(0), wout[g], preferred_element_type=f32)

                @pl.when(j == chunks - 1)
                def _():
                    for q in range(chips):
                        pair_copy(0, q).start()

                ig_acc[...] += contract_last(gathered(1), win[g])

    lax.fori_loop(0, chunks + 1 + 3 * (half - 1), step, None)

    for q in range(chips):
        pair_copy(1, q).start()
    for a, acc in enumerate((out_acc, ig_acc)):
        for q in range(chips):
            pair_copy(a, q).wait_recv()
        for k in range(chips):
            q = lax.rem(chip + k, chips)
            block = acc[token_rows(q, core), :] + pair[a, q]
            if k == 0:
                own_sum[a] = block
            else:
                others[k - 1][a] = block.astype(bf16)
        for q in range(chips):
            pair_copy(a, q).wait_send()

    for a in range(2):
        far_copy(a).wait()
        if a == 1:
            for k in range(1, chips):
                send_block(a, k).wait_send()
        for k in range(chips):
            share_block(a, k).wait_send()

    @pl.loop(0, chunks)
    def _(j):
        sum_copy(0, j).wait_send()
        sum_copy(1, j).wait_send()
        for copy in act_copies(j):
            copy.wait()

        @pl.when(has_outer)
        def _():
            result_copy(0, j).wait_send()
            result_copy(1, j).wait_send()


def layer(rows, cols, inputs, out_grad, w_in, w_out):
    tokens, feats = inputs.shape
    units = w_in.shape[1]
    chunks, batch = units // CHUNK, rows * tokens
    vmem = pl.BlockSpec(memory_space=pltpu.VMEM)
    far = pl.BlockSpec(memory_space=pl.ANY)
    dma = pltpu.SemaphoreType.DMA
    group = 2 if chunks % 2 == 0 else 1
    piece = (chunks, 2, batch, CHUNK)
    return pl.pallas_call(
        functools.partial(layer_kernel, rows, cols),
        out_shape=(
            jax.ShapeDtypeStruct((batch, feats), bf16),
            jax.ShapeDtypeStruct((batch, feats), bf16),
            jax.ShapeDtypeStruct((batch, units), bf16),
            jax.ShapeDtypeStruct((batch, units), bf16),
            jax.ShapeDtypeStruct((2, tokens, feats), f32),
        )
        + (jax.ShapeDtypeStruct((2, tokens, feats), bf16),) * (rows // 2 - 1),
        in_specs=[vmem, vmem, far, far],
        out_specs=[far] * 4 + [vmem] * (rows // 2),
        scratch_shapes=[
            pltpu.VMEM((batch, feats), bf16),
            pltpu.VMEM((batch, feats), bf16),
            pltpu.VMEM((batch, feats), f32),
            pltpu.VMEM((batch, feats), f32),
            pltpu.VMEM((2, rows // 2, tokens, feats), f32),
            pltpu.VMEM((2, rows, tokens, feats), bf16),
            pltpu.VMEM((chunks // group, feats, group * CHUNK), bf16),
            pltpu.VMEM((chunks // group, group * CHUNK, feats), bf16),
            pltpu.VMEM(piece, bf16),
            pltpu.VMEM(piece, bf16),
            pltpu.VMEM(piece, bf16),
            pltpu.VMEM((2, 2, batch, CHUNK), f32),
            pltpu.VMEM(((chunks + 1) // 2, batch, CHUNK), f32),
            dma((2, rows // 2)),
            dma((2, rows)),
            dma((2, rows // 2)),
            dma((2, chunks)),
            dma((2, chunks)),
            dma((2, chunks)),
            dma((2, chunks)),
            dma((2, chunks)),
            dma((2,)),
            dma((2, chunks)),
            dma((2, rows // 2)),
            dma((2, rows // 2)),
        ],
        compiler_params=pltpu.CompilerParams(
            collective_id=0, has_side_effects=True, vmem_limit_bytes=VMEM_BYTES
        ),
        cost_estimate=pl.CostEstimate(
            flops=8 * batch * feats * units, bytes_accessed=4 * feats * units, transcendentals=0
        ),
    )(inputs, out_grad, w_in, w_out)


def grad_kernel(left, right, out, turned):
    @pl.when(pl.program_id(0) == 0)
    def _():
        turned[...] = left[...].T

    out[...] = jnp.dot(turned[...], right[...], preferred_element_type=f32).astype(bf16)


def weight_grad(left, right):
    batch, height = left.shape
    width = right.shape[1]
    return pl.pallas_call(
        grad_kernel,
        grid=(width // CHUNK,),
        out_shape=jax.ShapeDtypeStruct((height, width), bf16),
        in_specs=[
            pl.BlockSpec((batch, height), lambda i: (0, 0)),
            pl.BlockSpec((batch, CHUNK), lambda i: (0, i)),
        ],
        out_specs=pl.BlockSpec((height, CHUNK), lambda i: (0, i)),
        scratch_shapes=[pltpu.VMEM((height, batch), bf16)],
        compiler_params=pltpu.CompilerParams(vmem_limit_bytes=VMEM_BYTES),
        cost_estimate=pl.CostEstimate(
            flops=2 * batch * height * width, bytes_accessed=2 * height * width, transcendentals=0
        ),
    )(left, right)


def local(rows, cols, inputs, w_in, w_out, out_grad):
    tokens, feats = inputs.shape
    chips = rows // 2
    x, og, act, hg, total, *blocks = layer(rows, cols, inputs, out_grad, w_in, w_out)

    for k in range(1, chips):
        shift = [(r, (r + 2 * k) % rows) for r in range(rows)]
        total = total + lax.ppermute(blocks[k - 1], "row", shift).astype(f32)
    total = total.astype(bf16)

    grad_out_w = weight_grad(act, og)
    grad_in_w = weight_grad(x, hg)
    return (total[0], total[1], grad_in_w, grad_out_w)


def solution(mesh):
    placed = (P("row", "col"), P("col", "row"), P("row", "col"), P("row", "col"))
    return jax.shard_map(
        functools.partial(local, mesh.shape["row"], mesh.shape["col"]),
        mesh=mesh,
        in_specs=placed,
        out_specs=(P("row", "col"), P("row", "col"), P("col", "row"), P("row", "col")),
        check_vma=False,
    )
```

```python
import functools

import jax
import jax.numpy as jnp
from jax import lax
from jax.experimental import pallas as pl
from jax.experimental.pallas import tpu as pltpu
from jax.sharding import PartitionSpec as P

gelu_scale = 0.7978845608028654
gelu_cubic = 0.044715
MESH = pl.DeviceIdType.MESH
CHUNK = 256
f32, bf16 = jnp.float32, jnp.bfloat16


def gelu_parts(hidden):
    inner = gelu_scale * (hidden + gelu_cubic * hidden * hidden * hidden)
    tangent = jnp.tanh(inner)
    value = 0.5 * hidden * (1.0 + tangent)
    slopes = 0.5 * (1.0 + tangent) + 0.5 * hidden * (1.0 - tangent * tangent) * gelu_scale * (
        1.0 + 3.0 * gelu_cubic * hidden * hidden
    )
    return (value, slopes)


def contract_first(left, right):
    return lax.dot_general(left, right, (((0,), (0,)), ((), ())), preferred_element_type=f32)


def contract_last(left, right):
    return lax.dot_general(left, right, (((1,), (1,)), ((), ())), preferred_element_type=f32)


def layer_kernel(
    rows, cols, own_in, own_grad, w_in, w_out, *refs
):
    (x_far, og_far, act, hg, own_sum), others = refs[:5], refs[5 : 4 + rows // 2]
    (
        x, og, out_acc, ig_acc, pair,
        slab, win, wout, from_outer, from_inner, to_inner, kept, early,
        gather_send, gather_recv, share_send, w_sem, outer_sem, inner_sem, in_send, out_send,
        far_sem, act_sem, pair_send, pair_recv,
    ) = refs[4 + rows // 2 :]
    row, col = lax.axis_index("row"), lax.axis_index("col")
    chips, half = rows // 2, cols // 2
    chip, core = row // 2, row % 2
    sibling = chip * 2 + (1 - core)
    chunks, tokens = win.shape[0], own_in.shape[0]

    lower = col < half
    inner = jnp.where(lower, col + 1, col - 1)
    outer = jnp.where(lower, col - 1, col + 1)
    away = jnp.where(lower, half - 1 - col, col - half)
    is_mid = away == 0
    has_outer = away < half - 1

    def weight_copies(j):
        cut = pl.ds(pl.multiple_of(j * CHUNK, CHUNK), CHUNK)
        return (
            pltpu.make_async_copy(w_in.at[:, cut], win.at[j], w_sem.at[0, j]),
            pltpu.make_async_copy(w_out.at[cut, :], wout.at[j], w_sem.at[1, j]),
        )

    barrier = pltpu.get_barrier_semaphore()
    for k in range(1, chips):
        there = lax.rem(chip + k, chips) * 2 + core
        pl.semaphore_signal(barrier, inc=1, device_id=(there, col), device_id_type=MESH)
    pl.semaphore_signal(barrier, inc=1, device_id=(sibling, col), device_id_type=MESH)
    pl.semaphore_signal(barrier, inc=1, device_id=(row, inner), device_id_type=MESH)

    @pl.when(has_outer)
    def _():
        pl.semaphore_signal(barrier, inc=1, device_id=(row, outer), device_id_type=MESH)

    @pl.loop(0, chunks)
    def _(j):
        for copy in weight_copies(j):
            copy.start()

    @pl.when(has_outer)
    def _():
        pl.semaphore_wait(barrier, chips + 2)

    @pl.when(jnp.logical_not(has_outer))
    def _():
        pl.semaphore_wait(barrier, chips + 1)

    own = (own_in, own_grad)

    def send_block(a, k):
        there = lax.rem(chip + k, chips) * 2 + core
        return pltpu.make_async_remote_copy(
            src_ref=own[a], dst_ref=slab.at[a, row], send_sem=gather_send.at[a, k],
            recv_sem=gather_recv.at[a, row], device_id=(there, col), device_id_type=MESH,
        )

    def share_block(a, k):
        source = lax.rem(chip + chips - k, chips) * 2 + core
        return pltpu.make_async_remote_copy(
            src_ref=own[a] if k == 0 else slab.at[a, source], dst_ref=slab.at[a, source],
            send_sem=share_send.at[a, k], recv_sem=gather_recv.at[a, source],
            device_id=(sibling, col), device_id_type=MESH,
        )

    def arrived(a, source):
        pltpu.make_async_remote_copy(
            src_ref=own[a], dst_ref=slab.at[a, source], send_sem=gather_send.at[a, 0],
            recv_sem=gather_recv.at[a, source], device_id=(sibling, col), device_id_type=MESH,
        ).wait_recv()

    def far_copy(a):
        return pltpu.make_async_copy((x, og)[a], (x_far, og_far)[a], far_sem.at[a])

    def early_step(s, _):
        weight_copies(s)[0].wait()
        early[s] = jnp.dot(x[...], win[s], preferred_element_type=f32)

    for k in range(1, chips):
        send_block(0, k).start()
    share_block(0, 0).start()
    for k in range(1, chips):
        send_block(0, k).wait_send()
    for k in range(1, chips):
        send_block(1, k).start()
    share_block(1, 0).start()
    for a, (whole, wide) in enumerate(((x, out_acc), (og, ig_acc))):
        for k in range(1, chips):
            arrived(a, lax.rem(chip + chips - k, chips) * 2 + core)
            share_block(a, k).start()
        for k in range(chips):
            arrived(a, lax.rem(chip + chips - k, chips) * 2 + 1 - core)

        def unfold(r, _, a=a, wide=wide):
            at = pl.ds(pl.multiple_of(r * tokens, 8), tokens)

            @pl.when(r == row)
            def _():
                wide[at, :] = own[a][...].astype(f32)

            @pl.when(r != row)
            def _():
                wide[at, :] = slab[a, r].astype(f32)

        lax.fori_loop(0, rows, unfold, None)
        whole[...] = wide[...].astype(bf16)
        wide[...] = jnp.zeros_like(wide)
        far_copy(a).start()
        if a == 0:
            lax.fori_loop(0, early.shape[0], early_step, None)

    def sum_copy(j):
        return pltpu.make_async_remote_copy(
            src_ref=to_inner.at[j], dst_ref=from_outer.at[j], send_sem=in_send.at[j],
            recv_sem=outer_sem.at[j], device_id=(row, inner), device_id_type=MESH,
        )

    def middle_copy(j):
        return pltpu.make_async_remote_copy(
            src_ref=to_inner.at[j], dst_ref=from_inner.at[j], send_sem=in_send.at[j],
            recv_sem=inner_sem.at[j], device_id=(row, inner), device_id_type=MESH,
        )

    def result_copy(j):
        return pltpu.make_async_remote_copy(
            src_ref=from_inner.at[j], dst_ref=from_inner.at[j], send_sem=out_send.at[j],
            recv_sem=inner_sem.at[j], device_id=(row, outer), device_id_type=MESH,
        )

    def act_copies(j):
        cut = pl.ds(pl.multiple_of(j * CHUNK, CHUNK), CHUNK)
        return tuple(
            pltpu.make_async_copy(from_inner.at[j, a], far.at[:, cut], act_sem.at[a, j])
            for a, far in enumerate((act, hg))
        )

    def token_rows(q, which):
        return pl.ds(pl.multiple_of((q * 2 + which) * tokens, 8), tokens)

    def pair_copy(a, q):
        return pltpu.make_async_remote_copy(
            src_ref=(out_acc, ig_acc)[a].at[token_rows(q, 1 - core), :], dst_ref=pair.at[a, q],
            send_sem=pair_send.at[a, q], recv_sem=pair_recv.at[a, q],
            device_id=(sibling, col), device_id_type=MESH,
        )

    lag = 1 + 3 * away

    def step(s, _):
        @pl.when(s < chunks)
        def _():
            weight_copies(s)[1].wait()
            slot = lax.rem(s, 2)

            @pl.when(s < early.shape[0])
            def _():
                kept[slot, 0] = early[s]

            @pl.when(s >= early.shape[0])
            def _():
                weight_copies(s)[0].wait()
                kept[slot, 0] = jnp.dot(x[...], win[s], preferred_element_type=f32)

            kept[slot, 1] = contract_last(og[...], wout[s])

            @pl.when(has_outer)
            def _():
                sum_copy(s).wait_recv()
                kept[slot] = kept[slot] + from_outer[s].astype(f32)

            to_inner[s] = kept[slot].astype(bf16)

            @pl.when(is_mid)
            def _():
                middle_copy(s).start()

            @pl.when(jnp.logical_not(is_mid))
            def _():
                sum_copy(s).start()

        j = s - lag

        @pl.when((j >= 0) & (j < chunks))
        def _():
            middle_copy(j).wait_recv()

            @pl.when(is_mid)
            def _():
                total = kept[lax.rem(j, 2)] + from_inner[j].astype(f32)
                value, slopes = gelu_parts(total[0])
                from_inner[j, 0] = value.astype(bf16)
                from_inner[j, 1] = (total[1] * slopes).astype(bf16)

            @pl.when(has_outer)
            def _():
                result_copy(j).start()

            for copy in act_copies(j):
                copy.start()
            out_acc[...] += jnp.dot(from_inner[j, 0], wout[j], preferred_element_type=f32)

            @pl.when(j == chunks - 1)
            def _():
                for q in range(chips):
                    pair_copy(0, q).start()

            ig_acc[...] += contract_last(from_inner[j, 1], win[j])

    lax.fori_loop(0, chunks + 1 + 3 * (half - 1), step, None)

    for q in range(chips):
        pair_copy(1, q).start()
    for a, acc in enumerate((out_acc, ig_acc)):
        for q in range(chips):
            pair_copy(a, q).wait_recv()
        for k in range(chips):
            q = lax.rem(chip + k, chips)
            block = acc[token_rows(q, core), :] + pair[a, q]
            if k == 0:
                own_sum[a] = block
            else:
                others[k - 1][a] = block.astype(bf16)
        for q in range(chips):
            pair_copy(a, q).wait_send()

    for a in range(2):
        far_copy(a).wait()
        if a == 1:
            for k in range(1, chips):
                send_block(a, k).wait_send()
        for k in range(chips):
            share_block(a, k).wait_send()

    @pl.loop(0, chunks)
    def _(j):
        sum_copy(j).wait_send()
        for copy in act_copies(j):
            copy.wait()

        @pl.when(has_outer)
        def _():
            result_copy(j).wait_send()


def layer(rows, cols, inputs, out_grad, w_in, w_out):
    tokens, feats = inputs.shape
    units = w_in.shape[1]
    chunks, batch = units // CHUNK, rows * tokens
    vmem = pl.BlockSpec(memory_space=pltpu.VMEM)
    far = pl.BlockSpec(memory_space=pl.ANY)
    dma = pltpu.SemaphoreType.DMA
    piece = (chunks, 2, batch, CHUNK)
    return pl.pallas_call(
        functools.partial(layer_kernel, rows, cols),
        out_shape=(
            jax.ShapeDtypeStruct((batch, feats), bf16),
            jax.ShapeDtypeStruct((batch, feats), bf16),
            jax.ShapeDtypeStruct((batch, units), bf16),
            jax.ShapeDtypeStruct((batch, units), bf16),
            jax.ShapeDtypeStruct((2, tokens, feats), f32),
        )
        + (jax.ShapeDtypeStruct((2, tokens, feats), bf16),) * (rows // 2 - 1),
        in_specs=[vmem, vmem, far, far],
        out_specs=[far] * 4 + [vmem] * (rows // 2),
        scratch_shapes=[
            pltpu.VMEM((batch, feats), bf16),
            pltpu.VMEM((batch, feats), bf16),
            pltpu.VMEM((batch, feats), f32),
            pltpu.VMEM((batch, feats), f32),
            pltpu.VMEM((2, rows // 2, tokens, feats), f32),
            pltpu.VMEM((2, rows, tokens, feats), bf16),
            pltpu.VMEM((chunks, feats, CHUNK), bf16),
            pltpu.VMEM((chunks, CHUNK, feats), bf16),
            pltpu.VMEM(piece, bf16),
            pltpu.VMEM(piece, bf16),
            pltpu.VMEM(piece, bf16),
            pltpu.VMEM((2, 2, batch, CHUNK), f32),
            pltpu.VMEM(((chunks + 1) // 2, batch, CHUNK), f32),
            dma((2, rows // 2)),
            dma((2, rows)),
            dma((2, rows // 2)),
            dma((2, chunks)),
            dma((chunks,)),
            dma((chunks,)),
            dma((chunks,)),
            dma((chunks,)),
            dma((2,)),
            dma((2, chunks)),
            dma((2, rows // 2)),
            dma((2, rows // 2)),
        ],
        compiler_params=pltpu.CompilerParams(
            collective_id=0, has_side_effects=True, vmem_limit_bytes=64 * 1024 * 1024 - 65536
        ),
        cost_estimate=pl.CostEstimate(
            flops=8 * batch * feats * units, bytes_accessed=4 * feats * units, transcendentals=0
        ),
    )(inputs, out_grad, w_in, w_out)


def grad_kernel(left, right, out, turned):
    @pl.when(pl.program_id(0) == 0)
    def _():
        turned[...] = left[...].T

    out[...] = jnp.dot(turned[...], right[...], preferred_element_type=f32).astype(bf16)


def weight_grad(left, right):
    batch, height = left.shape
    width = right.shape[1]
    return pl.pallas_call(
        grad_kernel,
        grid=(width // CHUNK,),
        out_shape=jax.ShapeDtypeStruct((height, width), bf16),
        in_specs=[
            pl.BlockSpec((batch, height), lambda i: (0, 0)),
            pl.BlockSpec((batch, CHUNK), lambda i: (0, i)),
        ],
        out_specs=pl.BlockSpec((height, CHUNK), lambda i: (0, i)),
        scratch_shapes=[pltpu.VMEM((height, batch), bf16)],
        compiler_params=pltpu.CompilerParams(vmem_limit_bytes=48 * 1024 * 1024),
        cost_estimate=pl.CostEstimate(
            flops=2 * batch * height * width, bytes_accessed=2 * height * width, transcendentals=0
        ),
    )(left, right)


def local(rows, cols, inputs, w_in, w_out, out_grad):
    tokens, feats = inputs.shape
    chips = rows // 2
    x, og, act, hg, total, *blocks = layer(rows, cols, inputs, out_grad, w_in, w_out)

    for k in range(1, chips):
        shift = [(r, (r + 2 * k) % rows) for r in range(rows)]
        total = total + lax.ppermute(blocks[k - 1], "row", shift).astype(f32)
    total = total.astype(bf16)

    grad_out_w = weight_grad(act, og)
    grad_in_w = weight_grad(x, hg)
    return (total[0], total[1], grad_in_w, grad_out_w)


def solution(mesh):
    placed = (P("row", "col"), P("col", "row"), P("row", "col"), P("row", "col"))
    return jax.shard_map(
        functools.partial(local, mesh.shape["row"], mesh.shape["col"]),
        mesh=mesh,
        in_specs=placed,
        out_specs=(P("row", "col"), P("row", "col"), P("col", "row"), P("row", "col")),
        check_vma=False,
    )
```
